32 devices in a mesh: row: 4 (over z), col: 8 (over y, x, core).
Axes of the slice: x: 2, y: 2, z: 4, core: 2. Of those that a mesh axis runs over, the one named last changes fastest.
Arguments:
- front: bfloat16 [32, 4, 128, 16, 8, 128], P(None, 'row', None, None, 'col'), may hold values from -8 to 25, as said below
- child_tiles: bfloat16 [1024, 128, 128], P(('row', 'col')), may hold values from -6 to 6
- tile_map: int32 [1024, 2], P(('row', 'col')), may hold values from 0 to 127, as said below
Outputs:
- factored: float32 [32, 4, 128, 16, 8, 128], P(None, 'row', None, None, 'col')
The draws below stay inside these ranges and needn't reach their ends.
Inputs may be any that keep to these rules, and one draw needn't show every extreme that they name: The leading 2048 x 2048 block of front is symmetric positive definite. `tile_map`: each row names a parent row tile outside the first 16 row tiles; column tiles may be any, the panel's included. The owner of tile (i, j) is the device at row i % 4 and column j % 8; the 32 tiles of one device send at most 2 tiles to any one owner, and in every draw some owner receives 2 tiles from every device.
All inputs are finite; a program needn't handle non-finite values.
Results may differ from the reference program's by a relative error of at most 0.0013.
Values may be sent and summed in bfloat16 or wider, within the bound.
A program may use at most 384 MiB of HBM per device.

```python
import jax
import jax.numpy as jnp
from jax import lax

NF = 16384
PANEL = 2048
TILE = 128
CAP = 2
NT = 128
PT = 16
DEVS = 32
KTD = 32
N_ROW = 4
N_COL = 8


def draw_front(key, part):
    key = jax.random.fold_in(key, 11)
    keys = jax.random.split(key, 5)
    rest = NF - PANEL
    scales = jax.random.uniform(keys[0], (PANEL,), jnp.float32, 1.0, 2.0)
    spots = jax.random.uniform(keys[1], (PANEL,), jnp.float32) * 64.0
    upper = jnp.clip(jax.random.normal(keys[2], (PANEL, rest), jnp.float32), -6.0, 6.0)
    lower = 0.35 * jnp.clip(jax.random.normal(keys[3], (rest, PANEL), jnp.float32), -6.0, 6.0)
    trailing = jnp.clip(jax.random.normal(keys[4], (rest, rest), jnp.float32), -6.0, 6.0)
    kernel = scales[:, None] * scales[None, :] * jnp.exp(-jnp.abs(spots[:, None] - spots[None, :]))
    kernel = kernel + 20.0 * jnp.eye(PANEL, dtype=jnp.float32)
    whole = jnp.concatenate([jnp.concatenate([kernel, upper], 1), jnp.concatenate([lower, trailing], 1)], 0)
    return whole.reshape(NT // N_ROW, N_ROW, TILE, NT // N_COL, N_COL, TILE).astype(jnp.bfloat16)


def draw_tile_map(key, part):
    key = jax.random.fold_in(key, 5)
    keys = jax.random.split(key, 4)
    pair_count = DEVS * CAP
    weights = jax.random.randint(keys[0], (DEVS,), 0, 4) * 400
    busiest = jax.random.randint(keys[1], (), 0, DEVS)
    weights = jnp.where(jnp.arange(DEVS) == busiest, 4000, weights)
    offsets = jax.random.randint(keys[2], (DEVS,), 0, 1 << 20)
    pair_dest = jnp.arange(pair_count) // CAP
    rows_free = NT // N_ROW - PT // N_ROW
    cols_free = NT // N_COL - PT // N_COL
    cols_panel = PT // N_COL

    def one_sender(sender_key, sender):
        first_key, second_key = jax.random.split(sender_key)
        scores = (weights[pair_dest] + jax.random.randint(first_key, (pair_count,), 0, 1024)) * pair_count + jnp.arange(pair_count)
        _, chosen = lax.top_k(scores, KTD)
        chosen = jax.random.permutation(second_key, chosen)
        target = chosen // CAP
        within = chosen % CAP
        counter = sender * CAP + within + offsets[target]
        to_panel = counter % 4 == 0
        spot = counter % (rows_free * cols_free)
        spot_panel = counter // 4 % (rows_free * cols_panel)
        row_spot = jnp.where(to_panel, spot_panel // cols_panel, spot // cols_free)
        col_spot = jnp.where(to_panel, spot_panel % cols_panel, PT // N_COL + spot % cols_free)
        tile_row = (PT // N_ROW + row_spot) * N_ROW + target // N_COL
        tile_col = col_spot * N_COL + target % N_COL
        return jnp.stack([tile_row, tile_col], 1)
    result = jax.vmap(one_sender)(jax.random.split(keys[3], DEVS), jnp.arange(DEVS))
    return result.reshape(DEVS * KTD, 2).astype(jnp.int32)


def block_levels(key, dims, cuts, smallest, high):
    def one(dim, parts):
        draws = jax.random.uniform(jax.random.fold_in(jax.random.fold_in(key, 6), dim), (parts,), jnp.float32, smallest / len(cuts), high / len(cuts))
        return jnp.repeat(jnp.exp(draws), dims[dim] // parts).reshape((-1,) + (1,) * (len(dims) - dim - 1))

    factor_of = one(*cuts[0])
    for cut in cuts[1:]:
        factor_of = factor_of * one(*cut)
    return factor_of


def centred(own_key, shape, width, bound, cuts=(), kind=jnp.bfloat16):
    values = width * jax.random.normal(own_key, shape, jnp.float32)
    if cuts:
        values = values * block_levels(own_key, shape, cuts, -0.22, 0.18)
    return jnp.clip(values, -bound, bound).astype(kind)


def setup_inputs(seed: int = 0) -> dict:
    splits = jax.random.split(jax.random.key(seed), 4)
    return {
        "front": draw_front(jax.random.fold_in(splits[3], 71), 0),
        "child_tiles": centred(splits[1], (DEVS * KTD, TILE, TILE), 1.0, 6.0, ((0, 32),)),
        "tile_map": draw_tile_map(jax.random.fold_in(splits[3], 71), 0),
    }


def reference(front, child_tiles, tile_map):
    tiled = front.reshape(NT, TILE, NT, TILE).transpose(0, 2, 1, 3).astype(jnp.float32)
    blocks = child_tiles.reshape(DEVS, KTD, TILE, TILE)
    places = tile_map.reshape(DEVS, KTD, 2)

    def add_block(carry, item):
        pieces, where_to = item
        carry = carry.at[where_to[:, 0], where_to[:, 1]].add(pieces.astype(jnp.float32))
        return (carry, None)
    tiled, _ = lax.scan(add_block, tiled, (blocks, places))
    assembled = tiled.transpose(0, 2, 1, 3).reshape(NF, NF).astype(jnp.bfloat16)
    corner = assembled[:PANEL, :PANEL].astype(jnp.float32)
    lower_factor = jnp.linalg.cholesky(corner)
    below = lax.linalg.triangular_solve(lower_factor, assembled[PANEL:, :PANEL].astype(jnp.float32), left_side=False, lower=True, transpose_a=True)
    panel = jnp.concatenate([lower_factor, below], 0).astype(jnp.bfloat16)
    lower_rows = panel[PANEL:].astype(jnp.float32)
    trailing = assembled[PANEL:, PANEL:].astype(jnp.float32) - jnp.dot(lower_rows.astype(jnp.float32), lower_rows.T.astype(jnp.float32), preferred_element_type=jnp.float32)
    upper_zero = jnp.zeros((PANEL, NF - PANEL), jnp.float32)
    right_part = jnp.concatenate([upper_zero, trailing], 0)
    factored = jnp.concatenate([panel.astype(jnp.float32), right_part], 1)
    return factored.reshape(NT // N_ROW, N_ROW, TILE, NT // N_COL, N_COL, TILE)
```

```python
import functools

import jax
import jax.numpy as jnp
from jax import lax
from jax.experimental import pallas as pl
from jax.experimental.pallas import tpu as pltpu
from jax.sharding import PartitionSpec as P

PANEL = 2048
CAP = 2
TILE = 128
STEP = 256
SUB = 8
VMEM_LIMIT = 56 * 1024 * 1024
NN = (((1,), (0,)), ((), ()))
NT = (((1,), (1,)), ((), ()))


def split(x):
    high = x.astype(jnp.bfloat16)
    low = (x - high.astype(jnp.float32)).astype(jnp.bfloat16)
    return high, low


def dot3(x, y, dims):
    xh, xl = split(x)
    yh, yl = split(y)
    dot = functools.partial(lax.dot_general, dimension_numbers=dims, preferred_element_type=jnp.float32)
    return dot(xh, yh) + (dot(xh, yl) + dot(xl, yh))


def factor_tile(s):
    n = s.shape[0]
    groups = n // SUB
    rows = lax.broadcasted_iota(jnp.int32, (SUB, n), 0)
    lanes = lax.broadcasted_iota(jnp.int32, (SUB, n), 1)
    left = [s[g * SUB : (g + 1) * SUB, :] for g in range(groups)]
    right = [(lanes == rows + g * SUB).astype(jnp.float32) for g in range(groups)]
    for g in range(groups):
        base = g * SUB
        r, e = left[g], right[g]
        cols = [jnp.broadcast_to(r[:, base + m : base + m + 1], (SUB, n)) for m in range(SUB)]
        u = jnp.zeros_like(r)
        v = jnp.zeros_like(e)
        u_rows, v_rows = [], []
        for i in range(SUB):
            inv = lax.rsqrt(jnp.broadcast_to(cols[i][i : i + 1, :], (SUB, n)))
            scaled = cols[i] * inv
            ru = jnp.broadcast_to(r[i : i + 1, :], (SUB, n)) * inv
            rv = jnp.broadcast_to(e[i : i + 1, :], (SUB, n)) * inv
            u_rows.append(ru)
            v_rows.append(rv)
            u = jnp.where(rows == i, ru, u)
            v = jnp.where(rows == i, rv, v)
            if i + 1 < SUB:
                r = r - scaled * ru
                e = e - scaled * rv
                for m in range(i + 1, SUB):
                    cols[m] = cols[m] - scaled * jnp.broadcast_to(scaled[m : m + 1, :], (SUB, n))
        left[g], right[g] = u, v
        if g + 1 < groups:
            ut = u.T
            for h in range(g + 1, groups):
                part = ut[h * SUB : (h + 1) * SUB, :]
                sh, eh = left[h], right[h]
                for m in range(SUB):
                    c = jnp.broadcast_to(part[:, m : m + 1], (SUB, n))
                    sh = sh - c * u_rows[m]
                    eh = eh - c * v_rows[m]
                left[h], right[h] = sh, eh
    upper = jnp.concatenate(left, 0)
    inverse = jnp.concatenate(right, 0)
    ri = lax.broadcasted_iota(jnp.int32, (n, n), 0)
    ci = lax.broadcasted_iota(jnp.int32, (n, n), 1)
    return jnp.where(ri <= ci, upper, 0.0), jnp.where(ri >= ci, inverse, 0.0)


def factor_kernel(row_count, col_count, blocks_ref, lower_ref, high_ref, low_ref, work_ref, inv_ref, q_ref):
    corner_rows = PANEL // TILE // row_count
    corner_cols = PANEL // TILE // col_count
    steps = PANEL // STEP
    half = STEP // 2

    def place(index, _):
        ri, ci = index // col_count, index % col_count
        for a in range(corner_rows):
            for b in range(corner_cols):
                r0 = pl.multiple_of((a * row_count + ri) * TILE, TILE)
                c0 = pl.multiple_of((b * col_count + ci) * TILE, TILE)
                work_ref[pl.ds(r0, TILE), pl.ds(c0, TILE)] = blocks_ref[
                    index, a * TILE : (a + 1) * TILE, b * TILE : (b + 1) * TILE
                ].astype(jnp.float32)
        return 0

    lax.fori_loop(0, row_count * col_count, place, 0)
    lower_ref[...] = jnp.zeros_like(lower_ref)

    def step(k, _):
        at = pl.multiple_of(k * STEP, STEP)
        here = pl.ds(at, STEP)
        s11 = work_ref[pl.ds(at, half), pl.ds(at, half)]
        up11, inv11 = factor_tile(s11)
        s21 = work_ref[pl.ds(at + half, half), pl.ds(at, half)]
        l21 = dot3(s21, inv11, NT)
        s22 = work_ref[pl.ds(at + half, half), pl.ds(at + half, half)] - dot3(l21, l21, NT)
        up22, inv22 = factor_tile(s22)
        inv21 = -dot3(inv22, dot3(l21, inv11, NN), NN)
        inv_ref[:half, :half] = inv11
        inv_ref[:half, half:] = jnp.zeros((half, half), jnp.float32)
        inv_ref[half:, :half] = inv21
        inv_ref[half:, half:] = inv22
        lower_ref[pl.ds(at, half), pl.ds(at, half)] = up11.T.astype(jnp.bfloat16)
        lower_ref[pl.ds(at + half, half), pl.ds(at, half)] = l21.astype(jnp.bfloat16)
        lower_ref[pl.ds(at + half, half), pl.ds(at + half, half)] = up22.T.astype(jnp.bfloat16)

        def block_row(j, _):
            cols = pl.ds(pl.multiple_of(j * STEP, STEP), STEP)
            q = dot3(inv_ref[...], work_ref[here, cols], NN)
            q = jnp.where(j == k, inv_ref[...], q)
            work_ref[here, cols] = q
            high, low = split(q)
            q_ref[0:STEP, cols] = high
            q_ref[STEP : 2 * STEP, cols] = low
            q_ref[2 * STEP :, cols] = high
            return 0

        lax.fori_loop(0, steps, block_row, 0)

        def below(i, _):
            mine = pl.ds(pl.multiple_of(i * STEP, STEP), STEP)
            p = dot3(work_ref[mine, here], inv_ref[...], NT)
            high, low = split(p)
            lower_ref[mine, here] = high
            work_ref[mine, here] = jnp.zeros((STEP, STEP), jnp.float32)
            wide = jnp.concatenate([high, high, low], 1)
            width = 2 * STEP
            for j in range(PANEL // width):
                cols = slice(j * width, (j + 1) * width)
                work_ref[mine, cols] = work_ref[mine, cols] - jnp.dot(
                    wide, q_ref[:, cols], preferred_element_type=jnp.float32
                )
            return 0

        lax.fori_loop(k + 1, steps, below, 0)
        return 0

    lax.fori_loop(0, steps, step, 0)

    def finish(i, _):
        mine = pl.ds(pl.multiple_of(i * TILE, TILE), TILE)
        rows = lax.broadcasted_iota(jnp.int32, (TILE, STEP), 0) + i * TILE
        lanes = lax.broadcasted_iota(jnp.int32, (TILE, STEP), 1)
        for j in range(steps):
            cols = slice(j * STEP, (j + 1) * STEP)
            high, low = split(jnp.where(rows >= lanes + j * STEP, work_ref[mine, cols], 0.0))
            high_ref[mine, cols] = high
            low_ref[mine, cols] = low
        return 0

    lax.fori_loop(0, PANEL // TILE, finish, 0)


def factor_corner(blocks, row_count, col_count):
    return pl.pallas_call(
        functools.partial(factor_kernel, row_count, col_count),
        out_shape=(jax.ShapeDtypeStruct((PANEL, PANEL), jnp.bfloat16),) * 3,
        in_specs=[pl.BlockSpec(memory_space=pltpu.VMEM)],
        out_specs=(pl.BlockSpec(memory_space=pltpu.VMEM),) * 3,
        scratch_shapes=[
            pltpu.VMEM((PANEL, PANEL), jnp.float32),
            pltpu.VMEM((STEP, STEP), jnp.float32),
            pltpu.VMEM((3 * STEP, PANEL), jnp.bfloat16),
        ],
        compiler_params=pltpu.CompilerParams(vmem_limit_bytes=VMEM_LIMIT),
        cost_estimate=pl.CostEstimate(flops=200 * 10**9, bytes_accessed=32 << 20, transcendentals=0),
        name="factor_corner",
    )(blocks)


def solve_kernel(col_count, parts_ref, high_ref, low_ref, out_ref, x_ref):
    tiles = parts_ref.shape[2] // TILE
    for b in range(tiles):
        for c in range(col_count):
            j = b * col_count + c
            x_ref[:, j * TILE : (j + 1) * TILE] = parts_ref[c, :, b * TILE : (b + 1) * TILE]
    for n in range(PANEL // STEP):
        end = (n + 1) * STEP
        rows = slice(n * STEP, end)
        x = x_ref[:, :end]
        y = lax.dot_general(x, high_ref[rows, :end], NT, preferred_element_type=jnp.float32)
        y = y + lax.dot_general(x, low_ref[rows, :end], NT, preferred_element_type=jnp.float32)
        out_ref[:, rows] = y.astype(jnp.bfloat16)


def solve_rows(parts, high, low, skip):
    col_count, rows, width = parts.shape
    chunk = 256 if rows % 256 == 0 and skip % 256 == 0 else TILE
    first = skip // chunk
    whole = pl.BlockSpec((PANEL, PANEL), lambda s: (0, 0))
    return pl.pallas_call(
        functools.partial(solve_kernel, col_count),
        grid=((rows - skip) // chunk,),
        out_shape=jax.ShapeDtypeStruct((rows - skip, PANEL), jnp.bfloat16),
        in_specs=[pl.BlockSpec((col_count, chunk, width), lambda s: (0, s + first, 0)), whole, whole],
        out_specs=pl.BlockSpec((chunk, PANEL), lambda s: (s, 0)),
        scratch_shapes=[pltpu.VMEM((chunk, PANEL), jnp.bfloat16)],
        compiler_params=pltpu.CompilerParams(vmem_limit_bytes=VMEM_LIMIT),
        cost_estimate=pl.CostEstimate(
            flops=2 * (rows - skip) * PANEL * PANEL, bytes_accessed=(rows - skip) * PANEL * 4, transcendentals=0
        ),
        name="solve_rows",
    )(parts, high, low)


def trailing_kernel(
    corner_rows, corner_cols, group, starts, order, spots, xr_ref, xc_ref, front_ref, own_ref, child_ref, out_ref
):
    step = pl.program_id(0)
    first = corner_rows // group

    @pl.when(step < first)
    def _():
        out_ref[...] = jnp.zeros_like(out_ref)

    @pl.when(step >= first)
    def _():
        out_ref[...] = front_ref[...].astype(jnp.float32)
        for part in range(group):
            rows = pl.ds(part * TILE, TILE)
            a = step * group + part

            def add(p, _):
                out_ref[rows, spots[p], :] = out_ref[rows, spots[p], :] + child_ref[order[p]].astype(jnp.float32)
                return 0

            lax.fori_loop(starts[a], starts[a + 1], add, 0)
        columns = out_ref.shape[1]
        for start in range(corner_cols, columns, 2):
            width = min(2, columns - start)
            at = (start - corner_cols) * TILE
            update = lax.dot_general(
                xr_ref[...],
                xc_ref[at : at + width * TILE, :],
                NT,
                preferred_element_type=jnp.float32,
            )
            for w in range(width):
                b = start + w
                out_ref[:, b, :] = (
                    out_ref[:, b, :].astype(jnp.bfloat16).astype(jnp.float32)
                    - update[:, w * TILE : (w + 1) * TILE]
                )

    for b in range(corner_cols):
        out_ref[:, b, :] = own_ref[:, b * TILE : (b + 1) * TILE].astype(jnp.float32)


def trailing_update(row_panel, col_panel, front, own, child, starts, order, spots, corner_rows, corner_cols):
    rows, cols_local, _ = front.shape
    group = 2 if corner_rows % 2 == 0 and rows // TILE % 2 == 0 else 1
    chunk = group * TILE
    first = corner_rows // group
    whole = lambda x: pl.BlockSpec(x.shape, lambda s, *_: (0,) * x.ndim)
    return pl.pallas_call(
        functools.partial(trailing_kernel, corner_rows, corner_cols, group),
        out_shape=jax.ShapeDtypeStruct((rows, cols_local, TILE), jnp.float32),
        grid_spec=pltpu.PrefetchScalarGridSpec(
            num_scalar_prefetch=3,
            grid=(rows // chunk,),
            in_specs=[
                pl.BlockSpec((chunk, PANEL), lambda s, *_: (jnp.maximum(s - first, 0), 0)),
                whole(col_panel),
                pl.BlockSpec((chunk, cols_local, TILE), lambda s, *_: (s, 0, 0)),
                pl.BlockSpec((chunk, corner_cols * TILE), lambda s, *_: (s, 0)),
                whole(child),
            ],
            out_specs=pl.BlockSpec((chunk, cols_local, TILE), lambda s, *_: (s, 0, 0)),
        ),
        compiler_params=pltpu.CompilerParams(vmem_limit_bytes=VMEM_LIMIT),
        name="trailing_update",
    )(starts, order, spots, row_panel, col_panel, front, own, child)


def per_device(front, child_tiles, tile_map):
    rows_local = front.shape[0]
    cols_local = front.shape[3]
    row_count = lax.axis_size("row")
    col_count = lax.axis_size("col")
    device_count = row_count * col_count
    row_index = lax.axis_index("row")
    col_index = lax.axis_index("col")
    panel_tiles = PANEL // TILE
    corner_rows = panel_tiles // row_count
    corner_cols = panel_tiles // col_count
    width = corner_cols * TILE
    front4 = front.reshape(rows_local, TILE, cols_local, TILE)

    corner = front4[:corner_rows, :, :corner_cols, :].reshape(corner_rows * TILE, width)
    blocks = lax.all_gather(corner, ("row", "col"), axis=0)

    owners = tile_map[:, 0] % row_count * col_count + tile_map[:, 1] % col_count
    local_ids = tile_map[:, 0] // row_count * cols_local + tile_map[:, 1] // col_count
    owner_hits = (owners[:, None] == jnp.arange(device_count)[None, :]).astype(jnp.int32)
    slot_rank = jnp.sum(jnp.cumsum(owner_hits, 0) * owner_hits, 1) - 1
    slot_index = owners * CAP + slot_rank
    packed = jnp.zeros((device_count * CAP, TILE, TILE), jnp.bfloat16).at[slot_index].set(child_tiles)
    targets = jnp.full((device_count * CAP,), -1, jnp.int32).at[slot_index].set(local_ids)
    exchange = functools.partial(
        lax.all_to_all, axis_name=("row", "col"), split_axis=0, concat_axis=0, tiled=True
    )
    arrived = exchange(packed.reshape(device_count, CAP, TILE, TILE))
    ids = exchange(targets.reshape(device_count, CAP)).reshape(device_count * CAP)
    arrived = arrived.reshape(device_count * CAP, TILE, TILE)
    tile_rows = jnp.where(ids < 0, rows_local, ids // cols_local)
    tile_cols = jnp.where(ids < 0, 0, ids % cols_local)

    panel_ids = jnp.where((ids >= 0) & (tile_cols < corner_cols), tile_rows * corner_cols + tile_cols, -1)
    selector = (panel_ids[None, :] == jnp.arange(rows_local * corner_cols)[:, None]).astype(jnp.bfloat16)
    added = jnp.dot(
        selector, arrived.reshape(device_count * CAP, TILE * TILE), preferred_element_type=jnp.float32
    )
    added = added.reshape(rows_local, corner_cols, TILE, TILE).transpose(0, 2, 1, 3)
    panel_part = (front4[:, :, :corner_cols, :].astype(jnp.float32) + added).astype(jnp.bfloat16)
    panel_part = panel_part.reshape(rows_local * TILE, width)

    row_parts = lax.all_gather(panel_part, "col", axis=0)
    all_rows = lax.all_gather(panel_part.reshape(rows_local, TILE, width), "row", axis=1)
    by_col = all_rows.reshape(cols_local, col_count, TILE, width)
    by_col = by_col[corner_cols:].transpose(1, 0, 2, 3).reshape(col_count, (cols_local - corner_cols) * TILE, width)
    col_parts = lax.all_to_all(by_col, "col", split_axis=0, concat_axis=0, tiled=True)

    lower, high, low = factor_corner(blocks, row_count, col_count)
    row_panel = solve_rows(row_parts, high, low, corner_rows * TILE)
    col_panel = solve_rows(col_parts, high, low, 0)

    top = lax.dynamic_index_in_dim(
        lower.reshape(corner_rows, row_count, TILE, PANEL), row_index, 1, keepdims=False
    ).reshape(corner_rows * TILE, PANEL)
    own = jnp.concatenate(
        [
            lax.dynamic_index_in_dim(x.reshape(-1, corner_cols, col_count, TILE), col_index, 2, keepdims=False)
            for x in (top, row_panel)
        ],
        0,
    ).reshape(rows_local * TILE, width)

    place = jnp.arange(device_count * CAP)
    before = (tile_rows[None, :] < tile_rows[:, None]) | (
        (tile_rows[None, :] == tile_rows[:, None]) & (place[None, :] < place[:, None])
    )
    rank = jnp.sum(before.astype(jnp.int32), 1)
    picked = (rank[None, :] == place[:, None]).astype(jnp.int32)
    order = jnp.sum(picked * place[None, :], 1)
    spots = jnp.sum(picked * tile_cols[None, :], 1)
    starts = jnp.sum((tile_rows[None, :] < jnp.arange(rows_local + 1)[:, None]).astype(jnp.int32), 1)
    result = trailing_update(
        row_panel,
        col_panel,
        front.reshape(rows_local * TILE, cols_local, TILE),
        own,
        arrived,
        starts,
        order,
        spots,
        corner_rows,
        corner_cols,
    )
    return result.reshape(rows_local, 1, TILE, cols_local, 1, TILE)


def solution(mesh):
    in_specs = (
        P(None, "row", None, None, "col", None),
        P(("row", "col"), None, None),
        P(("row", "col"), None),
    )
    out_specs = P(None, "row", None, None, "col", None)
    return jax.shard_map(
        per_device, mesh=mesh, in_specs=in_specs, out_specs=out_specs, check_vma=False
    )
```

```python
import functools

import jax
import jax.numpy as jnp
from jax import lax
from jax.experimental import pallas as pl
from jax.experimental.pallas import tpu as pltpu
from jax.sharding import PartitionSpec as P

PANEL = 2048
CAP = 2
TILE = 128
STEP = 256
SUB = 8
VMEM_LIMIT = 56 * 1024 * 1024
NN = (((1,), (0,)), ((), ()))
NT = (((1,), (1,)), ((), ()))


def split(x):
    high = x.astype(jnp.bfloat16)
    low = (x - high.astype(jnp.float32)).astype(jnp.bfloat16)
    return high, low


def dot3(x, y, dims):
    xh, xl = split(x)
    yh, yl = split(y)
    dot = functools.partial(lax.dot_general, dimension_numbers=dims, preferred_element_type=jnp.float32)
    return dot(xh, yh) + (dot(xh, yl) + dot(xl, yh))


def factor_tile(s):
    n = s.shape[0]
    groups = n // SUB
    rows = lax.broadcasted_iota(jnp.int32, (SUB, n), 0)
    lanes = lax.broadcasted_iota(jnp.int32, (SUB, n), 1)
    left = [s[g * SUB : (g + 1) * SUB, :] for g in range(groups)]
    right = [(lanes == rows + g * SUB).astype(jnp.float32) for g in range(groups)]
    for g in range(groups):
        base = g * SUB
        r, e = left[g], right[g]
        cols = [jnp.broadcast_to(r[:, base + m : base + m + 1], (SUB, n)) for m in range(SUB)]
        u = jnp.zeros_like(r)
        v = jnp.zeros_like(e)
        u_rows, v_rows = [], []
        for i in range(SUB):
            inv = lax.rsqrt(jnp.broadcast_to(cols[i][i : i + 1, :], (SUB, n)))
            scaled = cols[i] * inv
            ru = jnp.broadcast_to(r[i : i + 1, :], (SUB, n)) * inv
            rv = jnp.broadcast_to(e[i : i + 1, :], (SUB, n)) * inv
            u_rows.append(ru)
            v_rows.append(rv)
            u = jnp.where(rows == i, ru, u)
            v = jnp.where(rows == i, rv, v)
            if i + 1 < SUB:
                r = r - scaled * ru
                e = e - scaled * rv
                for m in range(i + 1, SUB):
                    cols[m] = cols[m] - scaled * jnp.broadcast_to(scaled[m : m + 1, :], (SUB, n))
        left[g], right[g] = u, v
        if g + 1 < groups:
            ut = u.T
            for h in range(g + 1, groups):
                part = ut[h * SUB : (h + 1) * SUB, :]
                sh, eh = left[h], right[h]
                for m in range(SUB):
                    c = jnp.broadcast_to(part[:, m : m + 1], (SUB, n))
                    sh = sh - c * u_rows[m]
                    eh = eh - c * v_rows[m]
                left[h], right[h] = sh, eh
    upper = jnp.concatenate(left, 0)
    inverse = jnp.concatenate(right, 0)
    ri = lax.broadcasted_iota(jnp.int32, (n, n), 0)
    ci = lax.broadcasted_iota(jnp.int32, (n, n), 1)
    return jnp.where(ri <= ci, upper, 0.0), jnp.where(ri >= ci, inverse, 0.0)


def factor_kernel(row_count, col_count, blocks_ref, lower_ref, high_ref, low_ref, work_ref, inv_ref, q_ref):
    corner_rows = PANEL // TILE // row_count
    corner_cols = PANEL // TILE // col_count
    steps = PANEL // STEP
    half = STEP // 2

    def place(index, _):
        ri, ci = index // col_count, index % col_count
        for a in range(corner_rows):
            for b in range(corner_cols):
                r0 = pl.multiple_of((a * row_count + ri) * TILE, TILE)
                c0 = pl.multiple_of((b * col_count + ci) * TILE, TILE)
                work_ref[pl.ds(r0, TILE), pl.ds(c0, TILE)] = blocks_ref[
                    index, a * TILE : (a + 1) * TILE, b * TILE : (b + 1) * TILE
                ].astype(jnp.float32)
        return 0

    lax.fori_loop(0, row_count * col_count, place, 0)
    lower_ref[...] = jnp.zeros_like(lower_ref)

    def step(k, _):
        at = pl.multiple_of(k * STEP, STEP)
        here = pl.ds(at, STEP)
        s11 = work_ref[pl.ds(at, half), pl.ds(at, half)]
        up11, inv11 = factor_tile(s11)
        s21 = work_ref[pl.ds(at + half, half), pl.ds(at, half)]
        l21 = dot3(s21, inv11, NT)
        s22 = work_ref[pl.ds(at + half, half), pl.ds(at + half, half)] - dot3(l21, l21, NT)
        up22, inv22 = factor_tile(s22)
        inv21 = -dot3(inv22, dot3(l21, inv11, NN), NN)
        inv_ref[:half, :half] = inv11
        inv_ref[:half, half:] = jnp.zeros((half, half), jnp.float32)
        inv_ref[half:, :half] = inv21
        inv_ref[half:, half:] = inv22
        lower_ref[pl.ds(at, half), pl.ds(at, half)] = up11.T.astype(jnp.bfloat16)
        lower_ref[pl.ds(at + half, half), pl.ds(at, half)] = l21.astype(jnp.bfloat16)
        lower_ref[pl.ds(at + half, half), pl.ds(at + half, half)] = up22.T.astype(jnp.bfloat16)

        def block_row(j, _):
            cols = pl.ds(pl.multiple_of(j * STEP, STEP), STEP)
            q = dot3(inv_ref[...], work_ref[here, cols], NN)
            q = jnp.where(j == k, inv_ref[...], q)
            work_ref[here, cols] = q
            high, low = split(q)
            q_ref[0:STEP, cols] = high
            q_ref[STEP : 2 * STEP, cols] = low
            q_ref[2 * STEP :, cols] = high
            return 0

        lax.fori_loop(0, steps, block_row, 0)

        def below(i, _):
            mine = pl.ds(pl.multiple_of(i * STEP, STEP), STEP)
            p = dot3(work_ref[mine, here], inv_ref[...], NT)
            high, low = split(p)
            lower_ref[mine, here] = high
            work_ref[mine, here] = jnp.zeros((STEP, STEP), jnp.float32)
            wide = jnp.concatenate([high, high, low], 1)
            width = 2 * STEP
            for j in range(PANEL // width):
                cols = slice(j * width, (j + 1) * width)
                work_ref[mine, cols] = work_ref[mine, cols] - jnp.dot(
                    wide, q_ref[:, cols], preferred_element_type=jnp.float32
                )
            return 0

        lax.fori_loop(k + 1, steps, below, 0)
        return 0

    lax.fori_loop(0, steps, step, 0)

    def finish(i, _):
        mine = pl.ds(pl.multiple_of(i * TILE, TILE), TILE)
        rows = lax.broadcasted_iota(jnp.int32, (TILE, STEP), 0) + i * TILE
        lanes = lax.broadcasted_iota(jnp.int32, (TILE, STEP), 1)
        for j in range(steps):
            cols = slice(j * STEP, (j + 1) * STEP)
            high, low = split(jnp.where(rows >= lanes + j * STEP, work_ref[mine, cols], 0.0))
            high_ref[mine, cols] = high
            low_ref[mine, cols] = low
        return 0

    lax.fori_loop(0, PANEL // TILE, finish, 0)


def factor_corner(blocks, row_count, col_count):
    return pl.pallas_call(
        functools.partial(factor_kernel, row_count, col_count),
        out_shape=(jax.ShapeDtypeStruct((PANEL, PANEL), jnp.bfloat16),) * 3,
        in_specs=[pl.BlockSpec(memory_space=pltpu.VMEM)],
        out_specs=(pl.BlockSpec(memory_space=pltpu.VMEM),) * 3,
        scratch_shapes=[
            pltpu.VMEM((PANEL, PANEL), jnp.float32),
            pltpu.VMEM((STEP, STEP), jnp.float32),
            pltpu.VMEM((3 * STEP, PANEL), jnp.bfloat16),
        ],
        compiler_params=pltpu.CompilerParams(vmem_limit_bytes=VMEM_LIMIT),
        cost_estimate=pl.CostEstimate(flops=200 * 10**9, bytes_accessed=32 << 20, transcendentals=0),
        name="factor_corner",
    )(blocks)


def solve_kernel(col_count, parts_ref, high_ref, low_ref, out_ref, x_ref):
    tiles = parts_ref.shape[2] // TILE
    for b in range(tiles):
        for c in range(col_count):
            j = b * col_count + c
            x_ref[:, j * TILE : (j + 1) * TILE] = parts_ref[c, :, b * TILE : (b + 1) * TILE]
    for n in range(PANEL // STEP):
        end = (n + 1) * STEP
        rows = slice(n * STEP, end)
        x = x_ref[:, :end]
        y = lax.dot_general(x, high_ref[rows, :end], NT, preferred_element_type=jnp.float32)
        y = y + lax.dot_general(x, low_ref[rows, :end], NT, preferred_element_type=jnp.float32)
        out_ref[:, rows] = y.astype(jnp.bfloat16)


def solve_rows(parts, high, low, skip):
    col_count, rows, width = parts.shape
    chunk = 256 if rows % 256 == 0 and skip % 256 == 0 else TILE
    first = skip // chunk
    whole = pl.BlockSpec((PANEL, PANEL), lambda s: (0, 0))
    return pl.pallas_call(
        functools.partial(solve_kernel, col_count),
        grid=((rows - skip) // chunk,),
        out_shape=jax.ShapeDtypeStruct((rows - skip, PANEL), jnp.bfloat16),
        in_specs=[pl.BlockSpec((col_count, chunk, width), lambda s: (0, s + first, 0)), whole, whole],
        out_specs=pl.BlockSpec((chunk, PANEL), lambda s: (s, 0)),
        scratch_shapes=[pltpu.VMEM((chunk, PANEL), jnp.bfloat16)],
        compiler_params=pltpu.CompilerParams(vmem_limit_bytes=VMEM_LIMIT),
        cost_estimate=pl.CostEstimate(
            flops=2 * (rows - skip) * PANEL * PANEL, bytes_accessed=(rows - skip) * PANEL * 4, transcendentals=0
        ),
        name="solve_rows",
    )(parts, high, low)


def trailing_kernel(
    corner_rows, corner_cols, group, starts, order, spots, xr_ref, xc_ref, front_ref, own_ref, child_ref, out_ref
):
    step = pl.program_id(0)
    first = corner_rows // group

    @pl.when(step < first)
    def _():
        out_ref[...] = jnp.zeros_like(out_ref)

    @pl.when(step >= first)
    def _():
        out_ref[...] = front_ref[...].astype(jnp.float32)
        for part in range(group):
            rows = pl.ds(part * TILE, TILE)
            a = step * group + part

            def add(p, _):
                out_ref[rows, spots[p], :] = out_ref[rows, spots[p], :] + child_ref[order[p]].astype(jnp.float32)
                return 0

            lax.fori_loop(starts[a], starts[a + 1], add, 0)
        columns = out_ref.shape[1]
        for start in range(corner_cols, columns, 2):
            width = min(2, columns - start)
            at = (start - corner_cols) * TILE
            update = lax.dot_general(
                xr_ref[...],
                xc_ref[at : at + width * TILE, :],
                NT,
                preferred_element_type=jnp.float32,
            )
            for w in range(width):
                b = start + w
                out_ref[:, b, :] = (
                    out_ref[:, b, :].astype(jnp.bfloat16).astype(jnp.float32)
                    - update[:, w * TILE : (w + 1) * TILE]
                )

    for b in range(corner_cols):
        out_ref[:, b, :] = own_ref[:, b * TILE : (b + 1) * TILE].astype(jnp.float32)


def trailing_update(row_panel, col_panel, front, own, child, starts, order, spots, corner_rows, corner_cols):
    rows, cols_local, _ = front.shape
    group = 2 if corner_rows % 2 == 0 and rows // TILE % 2 == 0 else 1
    chunk = group * TILE
    first = corner_rows // group
    whole = lambda x: pl.BlockSpec(x.shape, lambda s, *_: (0,) * x.ndim)
    return pl.pallas_call(
        functools.partial(trailing_kernel, corner_rows, corner_cols, group),
        out_shape=jax.ShapeDtypeStruct((rows, cols_local, TILE), jnp.float32),
        grid_spec=pltpu.PrefetchScalarGridSpec(
            num_scalar_prefetch=3,
            grid=(rows // chunk,),
            in_specs=[
                pl.BlockSpec((chunk, PANEL), lambda s, *_: (jnp.maximum(s - first, 0), 0)),
                whole(col_panel),
                pl.BlockSpec((chunk, cols_local, TILE), lambda s, *_: (s, 0, 0)),
                pl.BlockSpec((chunk, corner_cols * TILE), lambda s, *_: (s, 0)),
                whole(child),
            ],
            out_specs=pl.BlockSpec((chunk, cols_local, TILE), lambda s, *_: (s, 0, 0)),
        ),
        compiler_params=pltpu.CompilerParams(vmem_limit_bytes=VMEM_LIMIT),
        name="trailing_update",
    )(starts, order, spots, row_panel, col_panel, front, own, child)


def per_device(front, child_tiles, tile_map):
    rows_local = front.shape[0]
    cols_local = front.shape[3]
    row_count = lax.axis_size("row")
    col_count = lax.axis_size("col")
    device_count = row_count * col_count
    row_index = lax.axis_index("row")
    col_index = lax.axis_index("col")
    panel_tiles = PANEL // TILE
    corner_rows = panel_tiles // row_count
    corner_cols = panel_tiles // col_count
    width = corner_cols * TILE
    front4 = front.reshape(rows_local, TILE, cols_local, TILE)

    corner = front4[:corner_rows, :, :corner_cols, :].reshape(corner_rows * TILE, width)
    blocks = lax.all_gather(corner, ("row", "col"), axis=0)

    owners = tile_map[:, 0] % row_count * col_count + tile_map[:, 1] % col_count
    local_ids = tile_map[:, 0] // row_count * cols_local + tile_map[:, 1] // col_count
    owner_hits = (owners[:, None] == jnp.arange(device_count)[None, :]).astype(jnp.int32)
    slot_rank = jnp.sum(jnp.cumsum(owner_hits, 0) * owner_hits, 1) - 1
    slot_index = owners * CAP + slot_rank
    packed = jnp.zeros((device_count * CAP, TILE, TILE), jnp.bfloat16).at[slot_index].set(child_tiles)
    targets = jnp.full((device_count * CAP,), -1, jnp.int32).at[slot_index].set(local_ids)
    exchange = functools.partial(
        lax.all_to_all, axis_name=("row", "col"), split_axis=0, concat_axis=0, tiled=True
    )
    arrived = exchange(packed.reshape(device_count, CAP, TILE, TILE))
    ids = exchange(targets.reshape(device_count, CAP)).reshape(device_count * CAP)
    arrived = arrived.reshape(device_count * CAP, TILE, TILE)
    tile_rows = jnp.where(ids < 0, rows_local, ids // cols_local)
    tile_cols = jnp.where(ids < 0, 0, ids % cols_local)

    panel_ids = jnp.where((ids >= 0) & (tile_cols < corner_cols), tile_rows * corner_cols + tile_cols, -1)
    selector = (panel_ids[None, :] == jnp.arange(rows_local * corner_cols)[:, None]).astype(jnp.bfloat16)
    added = jnp.dot(
        selector, arrived.reshape(device_count * CAP, TILE * TILE), preferred_element_type=jnp.float32
    )
    added = added.reshape(rows_local, corner_cols, TILE, TILE).transpose(0, 2, 1, 3)
    panel_part = (front4[:, :, :corner_cols, :].astype(jnp.float32) + added).astype(jnp.bfloat16)
    panel_part = panel_part.reshape(rows_local * TILE, width)

    panel_part, blocks = lax.optimization_barrier((panel_part, blocks))
    lower, high, low = factor_corner(blocks, row_count, col_count)

    row_parts = lax.all_gather(panel_part, "col", axis=0)
    all_rows = lax.all_gather(panel_part.reshape(rows_local, TILE, width), "row", axis=1)
    all_rows, lower, high, low = lax.optimization_barrier((all_rows, lower, high, low))
    by_col = all_rows.reshape(cols_local, col_count, TILE, width)
    by_col = by_col[corner_cols:].transpose(1, 0, 2, 3).reshape(col_count, (cols_local - corner_cols) * TILE, width)
    col_parts = lax.all_to_all(by_col, "col", split_axis=0, concat_axis=0, tiled=True)

    row_panel = solve_rows(row_parts, high, low, corner_rows * TILE)
    col_panel = solve_rows(col_parts, high, low, 0)

    top = lax.dynamic_index_in_dim(
        lower.reshape(corner_rows, row_count, TILE, PANEL), row_index, 1, keepdims=False
    ).reshape(corner_rows * TILE, PANEL)
    own = jnp.concatenate(
        [
            lax.dynamic_index_in_dim(x.reshape(-1, corner_cols, col_count, TILE), col_index, 2, keepdims=False)
            for x in (top, row_panel)
        ],
        0,
    ).reshape(rows_local * TILE, width)

    place = jnp.arange(device_count * CAP)
    before = (tile_rows[None, :] < tile_rows[:, None]) | (
        (tile_rows[None, :] == tile_rows[:, None]) & (place[None, :] < place[:, None])
    )
    rank = jnp.sum(before.astype(jnp.int32), 1)
    picked = (rank[None, :] == place[:, None]).astype(jnp.int32)
    order = jnp.sum(picked * place[None, :], 1)
    spots = jnp.sum(picked * tile_cols[None, :], 1)
    starts = jnp.sum((tile_rows[None, :] < jnp.arange(rows_local + 1)[:, None]).astype(jnp.int32), 1)
    result = trailing_update(
        row_panel,
        col_panel,
        front.reshape(rows_local * TILE, cols_local, TILE),
        own,
        arrived,
        starts,
        order,
        spots,
        corner_rows,
        corner_cols,
    )
    return result.reshape(rows_local, 1, TILE, cols_local, 1, TILE)


def solution(mesh):
    in_specs = (
        P(None, "row", None, None, "col", None),
        P(("row", "col"), None, None),
        P(("row", "col"), None),
    )
    out_specs = P(None, "row", None, None, "col", None)
    return jax.shard_map(
        per_device, mesh=mesh, in_specs=in_specs, out_specs=out_specs, check_vma=False
    )
```
